128 devices in a mesh: tm: 16 (over y_lo, x, core), head: 8 (over z, y_hi).
Axes of the slice: x: 4, y: 4 (y_hi: 2, y_lo: 2; y = y_hi * 2 + y_lo), z: 4, core: 2. Of those that a mesh axis runs over, the one named last changes fastest.
Arguments:
- queries: bfloat16 [32768, 3072], P('tm', 'head'), may hold values from -8 to 8
- keys: bfloat16 [32768, 3072], P('tm', 'head'), may hold values from -8 to 8
- values: bfloat16 [32768, 3072], P('tm', 'head'), may hold values from -6 to 6
- right_blocks: bfloat16 [24, 128, 128], P('head'), may hold values from -0.5 to 0.5
- left_blocks: bfloat16 [24, 128, 128], P('head'), may hold values from -0.5 to 0.5
- block_perm: int32 [24], replicated, may hold values from 0 to 23, each once
- reach: int32 [24], replicated, may hold values from 0 to 2, as said below
- grad_out: bfloat16 [32768, 3072], P('tm', 'head'), may hold values from -6 to 6
Outputs:
- projected: bfloat16 [32768, 3072], P('tm', 'head')
- d_queries: bfloat16 [32768, 3072], P('tm', 'head')
- d_keys: bfloat16 [32768, 3072], P('tm', 'head')
- d_values: bfloat16 [32768, 3072], P('tm', 'head')
- d_right: float32 [24, 128, 128], P('head')
- d_left: float32 [24, 128, 128], P('head')
The draws below stay inside these ranges and needn't reach their ends.
Inputs may be any that keep to these rules, and one draw needn't show every extreme that they name: At least one head has reach 2. `block_perm`: each block number once.
All inputs are finite; a program needn't handle non-finite values.
Results may differ from the reference program's by a relative error of at most 0.023.
Values may be sent and summed in bfloat16 or wider, within the bound.
No kernel may reach another device: no remote copies, remote signals or barrier semaphores. Data moves between devices by JAX's collectives and lax.ppermute only.
A program may use at most 192 MiB of HBM per device.

```python
import jax
import jax.numpy as jnp
from jax import lax

NB = 24
BLK = 128
D = 3072
TILE = 128
RADIUS = 2
FR_DEV = 4
NTILE = 4
NF = 64
TOKENS = 32768
N_TM = 16


def draw_queries(key, part):
    base_key = jax.random.fold_in(key, 1)
    base = jax.random.truncated_normal(base_key, -6.0, 6.0, (TOKENS, D), jnp.float32)
    return base.astype(jnp.bfloat16)


def draw_keys(key, part):
    base_key = jax.random.fold_in(key, 2)
    base = jax.random.truncated_normal(base_key, -6.0, 6.0, (TOKENS, D), jnp.float32)
    return base.astype(jnp.bfloat16)


def draw_reach(key, part):
    drawn = jax.random.randint(jax.random.fold_in(key, 5), (NB,), 0, RADIUS + 1)
    picked = jax.random.randint(jax.random.fold_in(key, 6), (), 0, NB)
    return jnp.where(jnp.arange(NB) == picked, RADIUS, drawn).astype(jnp.int32)


def steps_of(own_key, dims, split, least, top_value):
    gain = 1.0
    for dim, parts in split:
        steps = jax.random.uniform(jax.random.fold_in(jax.random.fold_in(own_key, 6), dim), (parts,), jnp.float32, least / len(split), top_value / len(split))
        gain = gain * jnp.repeat(jnp.exp(steps), dims[dim] // parts).reshape((-1,) + (1,) * (len(dims) - 1 - dim))
    return gain


def gaussian(key, extent, spread, most, pieces=(), kind=jnp.bfloat16):
    values = spread * jax.random.normal(key, extent, jnp.float32)
    if pieces:
        values = values * steps_of(key, extent, pieces, -0.22, 0.18)
    return jnp.clip(values, -most, most).astype(kind)


def setup_inputs(seed: int = 0) -> dict:
    seeds = jax.random.split(jax.random.key(seed), 9)
    return {
        "queries": draw_queries(jax.random.fold_in(seeds[8], 71), 0),
        "keys": draw_keys(jax.random.fold_in(seeds[8], 71), 0),
        "values": gaussian(seeds[2], (TOKENS, D), 1.0, 6.0, ((0, 16), (1, 8))),
        "right_blocks": gaussian(seeds[3], (NB, BLK, BLK), BLK ** -0.5, 0.5, ((0, 8),)),
        "left_blocks": gaussian(seeds[4], (NB, BLK, BLK), BLK ** -0.5, 0.5, ((0, 8),)),
        "block_perm": jax.random.permutation(seeds[5], NB).astype(jnp.int32),
        "reach": draw_reach(jax.random.fold_in(seeds[8], 71), 0),
        "grad_out": gaussian(seeds[7], (TOKENS, D), 1.0, 6.0, ((0, 16), (1, 8))),
    }


def stored(value):
    return lax.optimization_barrier(value.astype(jnp.bfloat16))


def frame_mask(reach_heads, frames_q, frames_k, total_frames):
    gap = jnp.abs(frames_q[:, None] - frames_k[None, :])
    valid_q = (frames_q >= 0) & (frames_q < total_frames)
    valid_k = (frames_k >= 0) & (frames_k < total_frames)
    inside = valid_q[:, None] & valid_k[None, :]
    return (gap[None, :, :] <= reach_heads[:, None, None]) & inside[None, :, :]


def frame_list(first, count):
    return first + jnp.arange(count * TILE, dtype=jnp.int32) // TILE


def take_rows(block, first, count, tile):
    piece = lax.dynamic_slice_in_dim(block, first, count, 0)
    piece = lax.dynamic_index_in_dim(piece, tile, 1, keepdims=False)
    return piece.reshape((count * TILE,) + piece.shape[2:])


def take_stats(block, first, count, tile):
    piece = lax.dynamic_slice_in_dim(block, first, count, 0)
    piece = lax.dynamic_index_in_dim(piece, tile, 1, keepdims=False)
    piece = jnp.transpose(piece, (1, 0, 2))
    return piece.reshape(piece.shape[0], count * TILE)


def scores(q_rows, k_rows, scale):
    return jnp.einsum('qhd,khd->hqk', q_rows.astype(jnp.float32), k_rows.astype(jnp.float32)) * scale


def attend(q_rows, k_rows, v_rows, allowed, scale):
    s = scores(q_rows, k_rows, scale)
    top = jnp.max(jnp.where(allowed, s, -jnp.inf), axis=2, keepdims=True)
    total = jnp.sum(jnp.where(allowed, jnp.exp(s - top), 0.0), axis=2, keepdims=True)
    lse = top + jnp.log(total)
    probs = stored(jnp.where(allowed, jnp.exp(s - lse), 0.0))
    out = jnp.einsum('hqk,khd->qhd', probs.astype(jnp.float32), v_rows.astype(jnp.float32))
    return stored(out), lse[:, :, 0]


def probs_again(q_rows, k_rows, allowed, lse, scale):
    s = scores(q_rows, k_rows, scale)
    return jnp.where(allowed, jnp.exp(s - lse[:, :, None]), 0.0)


def score_grads(probs, d_rows, v_rows, delta, scale):
    dp = jnp.einsum('qhd,khd->hqk', d_rows.astype(jnp.float32), v_rows.astype(jnp.float32))
    return stored(probs * (dp - delta[:, :, None]) * scale)


def reference(queries, keys, values, right_blocks, left_blocks, block_perm, reach, grad_out):
    f32 = jnp.float32
    scale = BLK ** -0.5
    span = FR_DEV + 2 * RADIUS
    shape5 = (NF, NTILE, TILE, NB, BLK)
    pad5 = ((RADIUS, RADIUS), (0, 0), (0, 0), (0, 0), (0, 0))
    pad4 = ((RADIUS, RADIUS), (0, 0), (0, 0), (0, 0))
    q5 = queries.reshape(shape5)
    k5 = keys.reshape(shape5)
    v5 = values.reshape(shape5)
    k_pad = jnp.pad(k5, pad5)
    v_pad = jnp.pad(v5, pad5)
    count = N_TM * NTILE
    order = jnp.arange(count, dtype=jnp.int32)

    def forward_block(index):
        first = (index // NTILE) * FR_DEV
        tile = index % NTILE
        allowed = frame_mask(reach, frame_list(first, FR_DEV), frame_list(first - RADIUS, span), NF)
        return attend(take_rows(q5, first, FR_DEV, tile), take_rows(k_pad, first, span, tile),
                      take_rows(v_pad, first, span, tile), allowed, scale)

    attn_blocks, lse_blocks = lax.map(forward_block, order)
    attn = jnp.transpose(attn_blocks.reshape(N_TM, NTILE, FR_DEV, TILE, NB, BLK), (0, 2, 1, 3, 4, 5)).reshape(TOKENS, NB, BLK)
    lse4 = jnp.transpose(lse_blocks.reshape(N_TM, NTILE, NB, FR_DEV, TILE), (0, 3, 1, 2, 4)).reshape(NF, NTILE, NB, TILE)

    mixed = stored(jnp.einsum('nbi,bij->nbj', attn.astype(f32), right_blocks.astype(f32)))
    placed = jnp.transpose(mixed[:, block_perm, :], (0, 2, 1)).reshape(TOKENS, NB, BLK)
    cot3 = grad_out.reshape(TOKENS, NB, BLK)
    projected = jnp.einsum('nci,cio->nco', placed.astype(f32), left_blocks.astype(f32)).astype(jnp.bfloat16).reshape(TOKENS, D)
    norm = TOKENS ** -0.5
    d_placed = stored(jnp.einsum('nco,cio->nci', cot3.astype(f32), left_blocks.astype(f32)))
    d_left = jnp.einsum('nci,nco->cio', placed.astype(f32), cot3.astype(f32)) * norm
    d_perm = jnp.transpose(d_placed.reshape(TOKENS, BLK, NB), (0, 2, 1))
    d_mixed = d_perm[:, jnp.argsort(block_perm), :]
    d_attn = stored(jnp.einsum('nbj,bij->nbi', d_mixed.astype(f32), right_blocks.astype(f32)))
    d_right = jnp.einsum('nbi,nbj->bij', attn.astype(f32), d_mixed.astype(f32)) * norm
    delta = jnp.sum(d_attn.astype(f32) * attn.astype(f32), axis=2)
    delta4 = jnp.transpose(delta.reshape(NF, NTILE, TILE, NB), (0, 1, 3, 2))

    d5 = d_attn.reshape(shape5)
    q_pad = jnp.pad(q5, pad5)
    d_pad = jnp.pad(d5, pad5)
    lse_pad = jnp.pad(lse4, pad4)
    delta_pad = jnp.pad(delta4, pad4)

    def backward_block(index):
        first = (index // NTILE) * FR_DEV
        tile = index % NTILE
        own_frames = frame_list(first, FR_DEV)
        ext_frames = frame_list(first - RADIUS, span)
        near = frame_mask(reach, own_frames, ext_frames, NF)
        far = frame_mask(reach, ext_frames, own_frames, NF)
        q_rows = take_rows(q5, first, FR_DEV, tile)
        d_rows = take_rows(d5, first, FR_DEV, tile)
        k_ext = take_rows(k_pad, first, span, tile)
        v_ext = take_rows(v_pad, first, span, tile)
        probs = probs_again(q_rows, k_ext, near, take_stats(lse4, first, FR_DEV, tile), scale)
        grads = score_grads(probs, d_rows, v_ext, take_stats(delta4, first, FR_DEV, tile), scale)
        d_query = jnp.einsum('hqk,khd->qhd', grads.astype(f32), k_ext.astype(f32)).astype(jnp.bfloat16)
        q_far = take_rows(q_pad, first, span, tile)
        d_far = take_rows(d_pad, first, span, tile)
        k_own = take_rows(k5, first, FR_DEV, tile)
        v_own = take_rows(v5, first, FR_DEV, tile)
        probs_far = probs_again(q_far, k_own, far, take_stats(lse_pad, first, span, tile), scale)
        grads_far = score_grads(probs_far, d_far, v_own, take_stats(delta_pad, first, span, tile), scale)
        d_key = jnp.einsum('hqk,qhd->khd', grads_far.astype(f32), q_far.astype(f32)).astype(jnp.bfloat16)
        probs_low = stored(probs_far)
        d_value = jnp.einsum('hqk,qhd->khd', probs_low.astype(f32), d_far.astype(f32)).astype(jnp.bfloat16)
        return d_query, d_key, d_value

    dq_blocks, dk_blocks, dv_blocks = lax.map(backward_block, order)

    def assemble(blocks):
        return jnp.transpose(blocks.reshape(N_TM, NTILE, FR_DEV, TILE, NB, BLK), (0, 2, 1, 3, 4, 5)).reshape(TOKENS, D)

    return projected, assemble(dq_blocks), assemble(dk_blocks), assemble(dv_blocks), d_right, d_left
```

```python
import functools

import jax
import jax.numpy as jnp
from jax import lax
from jax.experimental import pallas as pl
from jax.experimental.pallas import tpu as pltpu
from jax.sharding import PartitionSpec as P

NB = 24
BLK = 128
TILE = 128
RADIUS = 2
FR_DEV = 4
NTILE = 4
NF = 64
HL = 3
WID = HL * BLK
ROWS = FR_DEV * NTILE * TILE
COLS = FR_DEV * TILE
PIECE = 16
SCALE = BLK ** (-0.5)
LOG2E = 1.4426950408889634
NEG = -1e30
F32 = jnp.float32
BF16 = jnp.bfloat16
VMEM = 56 * 1024 * 1024

NN = (((1,), (0,)), ((), ()))
NT = (((1,), (1,)), ((), ()))
TN = (((0,), (0,)), ((), ()))


def dot(a, b, dims=NN):
    return lax.dot_general(a, b, dims, preferred_element_type=F32)


def params():
    return pltpu.CompilerParams(vmem_limit_bytes=VMEM, dimension_semantics=("arbitrary",))


def placer_of(perm_ref, flip):
    shape = (WID, 1) if flip else (1, WID)
    col = lax.broadcasted_iota(jnp.int32, shape, 0 if flip else 1)
    block = lax.rem(col, NB)
    lane = lax.div(col, NB)
    source = jnp.zeros(shape, jnp.int32)
    for b in range(NB):
        source = jnp.where(block == b, perm_ref[b] * PIECE, source)
    source = source + lane
    row = lax.broadcasted_iota(jnp.int32, (WID, WID), 1 if flip else 0)
    return jnp.where(row == source, 1.0, 0.0).astype(BF16)


def block_diag(blocks):
    rows = []
    for c in range(HL):
        parts = [blocks[c] if d == c else jnp.zeros((BLK, BLK), BF16) for d in range(HL)]
        rows.append(jnp.concatenate(parts, axis=1))
    return jnp.concatenate(rows, axis=0)


def piece_order():
    row = lax.broadcasted_iota(jnp.int32, (WID, WID), 0)
    col = lax.broadcasted_iota(jnp.int32, (WID, WID), 1)
    s = lax.div(col, HL * PIECE)
    rest = lax.rem(col, HL * PIECE)
    want = lax.div(rest, PIECE) * BLK + s * PIECE + lax.rem(rest, PIECE)
    return jnp.where(row == want, 1.0, 0.0).astype(BF16)


def prep_kernel(perm_ref, left_ref, right_ref, g_ref, w_ref, rb_ref, da_ref):
    @pl.when(pl.program_id(0) == 0)
    def _():
        w_ref[...] = dot(placer_of(perm_ref, False), block_diag(left_ref[...])).astype(BF16)
        rb_ref[...] = dot(block_diag(right_ref[...]), piece_order()).astype(BF16)

    g = g_ref[...].reshape(COLS, WID)
    da_ref[...] = dot(w_ref[...], g, NT).astype(BF16)


def whole(shape):
    return pl.BlockSpec(shape, lambda t: (0,) * len(shape))


def smem():
    return pl.BlockSpec(memory_space=pltpu.SMEM)


def tile_spec(frames):
    return pl.BlockSpec((frames, 1, TILE, WID), lambda t: (0, t, 0, 0))


def col_spec():
    return pl.BlockSpec((WID, COLS), lambda t: (0, t))


def prep(perm, left, right, g4):
    return pl.pallas_call(
        prep_kernel,
        grid=(NTILE,),
        in_specs=[smem(), whole((HL, BLK, BLK)), whole((HL, BLK, BLK)), tile_spec(FR_DEV)],
        out_specs=[whole((WID, WID)), whole((WID, WID)), col_spec()],
        out_shape=[
            jax.ShapeDtypeStruct((WID, WID), BF16),
            jax.ShapeDtypeStruct((WID, WID), BF16),
            jax.ShapeDtypeStruct((WID, ROWS), BF16),
        ],
        compiler_params=params(),
        cost_estimate=pl.CostEstimate(flops=10**9, bytes_accessed=4 * 10**6, transcendentals=0),
        name="prep",
    )(perm, left, right, g4)


def ext_rows(lo, own, hi, h, first, count):
    cols = slice(h * BLK, (h + 1) * BLK)
    parts = []
    for e in range(first, first + count):
        if e < RADIUS:
            parts.append(lo[e, 0, :, cols])
        elif e < RADIUS + FR_DEV:
            parts.append(own[e - RADIUS, 0, :, cols])
        else:
            parts.append(hi[e - RADIUS - FR_DEV, 0, :, cols])
    return jnp.concatenate(parts, axis=0)


SPAN = 6


def forward_kernel(
    reach_ref, q_ref, k_ref, v_ref, klo, khi, vlo, vhi, rb_ref, at_ref, p_ref, mix_ref
):
    base = lax.axis_index("tm") * FR_DEV
    head0 = lax.axis_index("head") * HL
    for h in range(HL):
        reach = reach_ref[head0 + h]
        cols = slice(h * BLK, (h + 1) * BLK)
        for pair in range(2):
            f0 = 2 * pair
            q = q_ref[f0 : f0 + 2, 0, :, cols].reshape(2 * TILE, BLK)
            k = ext_rows(klo, k_ref, khi, h, f0, SPAN)
            v = ext_rows(vlo, v_ref, vhi, h, f0, SPAN)
            s = dot(k, q, NT)
            halves = []
            for a in range(2):
                parts = []
                for j in range(5):
                    frame = base + f0 + a + j - RADIUS
                    ok = (abs(j - RADIUS) <= reach) & (frame >= 0) & (frame < NF)
                    bias = jnp.where(ok, 0.0, NEG)
                    e = a + j
                    piece = s[e * TILE : (e + 1) * TILE, a * TILE : (a + 1) * TILE]
                    parts.append(piece * (SCALE * LOG2E) + bias)
                x = jnp.concatenate(parts, axis=0)
                top = jnp.max(x, axis=0, keepdims=True)
                x = jnp.exp2(x - top)
                total = jnp.sum(x, axis=0, keepdims=True)
                x = (x * (1.0 / total)).astype(BF16)
                zero = jnp.zeros((TILE, TILE), BF16)
                halves.append(jnp.concatenate([x, zero] if a == 0 else [zero, x], axis=0))
            p = jnp.concatenate(halves, axis=1)
            p_ref[0, h, pair] = p
            at_ref[cols, f0 * TILE : (f0 + 2) * TILE] = dot(v, p, TN).astype(BF16)
    mix_ref[...] = dot(rb_ref[...], at_ref[...], TN).astype(BF16)


def forward(reach, q4, k4, v4, klo, khi, vlo, vhi, rb):
    return pl.pallas_call(
        forward_kernel,
        grid=(NTILE,),
        in_specs=[smem()]
        + [tile_spec(FR_DEV)] * 3
        + [tile_spec(RADIUS)] * 4
        + [whole((WID, WID))],
        out_specs=[
            col_spec(),
            pl.BlockSpec((1, HL, 2, SPAN * TILE, 2 * TILE), lambda t: (t, 0, 0, 0, 0)),
            col_spec(),
        ],
        out_shape=[
            jax.ShapeDtypeStruct((WID, ROWS), BF16),
            jax.ShapeDtypeStruct((NTILE, HL, 2, SPAN * TILE, 2 * TILE), BF16),
            jax.ShapeDtypeStruct((WID, ROWS), BF16),
        ],
        compiler_params=params(),
        cost_estimate=pl.CostEstimate(
            flops=6 * 10**9, bytes_accessed=20 * 10**6, transcendentals=4 * 10**6
        ),
        name="forward",
    )(reach, q4, k4, v4, klo, khi, vlo, vhi, rb)


def backward_kernel(
    q_ref, k_ref, v_ref, klo, khi, vlo, vhi, rb_ref, at_ref, p_ref, dm_ref,
    dq_ref, dk_ref, dv_ref, lo_ref, hi_ref, r_ref, acc_ref,
):
    t = pl.program_id(0)
    dat = dot(rb_ref[...], dm_ref[...]).astype(BF16)
    term = dot(at_ref[...], dm_ref[...], NT)

    @pl.when(t == 0)
    def _():
        acc_ref[...] = term

    @pl.when(t > 0)
    def _():
        acc_ref[...] += term

    for h in range(HL):
        cols = slice(h * BLK, (h + 1) * BLK)
        dat_h = dat[cols, :]
        delta = jnp.sum(dat_h.astype(F32) * at_ref[cols, :].astype(F32), axis=0, keepdims=True)
        dks, dvs = [], []
        for pair in range(2):
            f0 = 2 * pair
            lanes = slice(f0 * TILE, (f0 + 2) * TILE)
            q = q_ref[f0 : f0 + 2, 0, :, cols].reshape(2 * TILE, BLK)
            k = ext_rows(klo, k_ref, khi, h, f0, SPAN)
            v = ext_rows(vlo, v_ref, vhi, h, f0, SPAN)
            p = p_ref[0, h, pair]
            d_t = dat_h[:, lanes]
            dp = dot(v, d_t)
            grads = (p.astype(F32) * (dp - delta[:, lanes])).astype(BF16)
            dq = dot(grads, k, TN) * SCALE
            dq_ref[f0 : f0 + 2, 0, :, cols] = dq.astype(BF16).reshape(2, TILE, BLK)
            dks.append(dot(grads, q) * SCALE)
            dvs.append(dot(p, d_t, NT))
        for which, (low, high) in enumerate((dks, dvs)):
            own_ref = dk_ref if which == 0 else dv_ref
            for e in range(RADIUS):
                lo_ref[which, e, 0, :, cols] = low[e * TILE : (e + 1) * TILE].astype(BF16)
                hi_ref[which, e, 0, :, cols] = high[(e + 4) * TILE : (e + 5) * TILE].astype(BF16)
            for e in range(FR_DEV):
                own = low[(e + 2) * TILE : (e + 3) * TILE] + high[e * TILE : (e + 1) * TILE]
                own_ref[e, 0, :, cols] = own.astype(BF16)

    @pl.when(t == NTILE - 1)
    def _():
        full = dot(acc_ref[...].astype(BF16), piece_order(), NT)
        for b in range(HL):
            r_ref[b] = full[b * BLK : (b + 1) * BLK, b * BLK : (b + 1) * BLK].astype(BF16)


def backward(q4, k4, v4, klo, khi, vlo, vhi, rb, attn_t, probs, dmix):
    out4 = jax.ShapeDtypeStruct((FR_DEV, NTILE, TILE, WID), BF16)
    halo = jax.ShapeDtypeStruct((2, RADIUS, NTILE, TILE, WID), BF16)
    halo_spec = pl.BlockSpec((2, RADIUS, 1, TILE, WID), lambda t: (0, 0, t, 0, 0))
    return pl.pallas_call(
        backward_kernel,
        grid=(NTILE,),
        in_specs=[tile_spec(FR_DEV)] * 3
        + [tile_spec(RADIUS)] * 4
        + [
            whole((WID, WID)),
            col_spec(),
            pl.BlockSpec((1, HL, 2, SPAN * TILE, 2 * TILE), lambda t: (t, 0, 0, 0, 0)),
            col_spec(),
        ],
        out_specs=[tile_spec(FR_DEV)] * 3 + [halo_spec] * 2 + [whole((HL, BLK, BLK))],
        out_shape=[out4] * 3 + [halo] * 2 + [jax.ShapeDtypeStruct((HL, BLK, BLK), BF16)],
        scratch_shapes=[pltpu.VMEM((WID, WID), F32)],
        compiler_params=params(),
        cost_estimate=pl.CostEstimate(
            flops=12 * 10**9, bytes_accessed=30 * 10**6, transcendentals=0
        ),
        name="backward",
    )(q4, k4, v4, klo, khi, vlo, vhi, rb, attn_t, probs, dmix)


def add_kernel(dk_ref, dv_ref, below_ref, above_ref, ok_ref, ov_ref):
    for which, (own, out) in enumerate(((dk_ref, ok_ref), (dv_ref, ov_ref))):
        for e in range(RADIUS):
            out[e] = (own[e].astype(F32) + below_ref[which, e].astype(F32)).astype(BF16)
            up = own[RADIUS + e].astype(F32) + above_ref[which, e].astype(F32)
            out[RADIUS + e] = up.astype(BF16)


def add_halos(dk, dv, below, above):
    halo_spec = pl.BlockSpec((2, RADIUS, 1, TILE, WID), lambda t: (0, 0, t, 0, 0))
    out4 = jax.ShapeDtypeStruct((FR_DEV, NTILE, TILE, WID), BF16)
    return pl.pallas_call(
        add_kernel,
        grid=(NTILE,),
        in_specs=[tile_spec(FR_DEV)] * 2 + [halo_spec] * 2,
        out_specs=[tile_spec(FR_DEV)] * 2,
        out_shape=[out4] * 2,
        compiler_params=params(),
        cost_estimate=pl.CostEstimate(flops=10**6, bytes_accessed=10 * 10**6, transcendentals=0),
        name="add_halos",
    )(dk, dv, below, above)


def project_kernel(perm_ref, w_ref, arr_ref, g_ref, out_ref, l_ref, acc_ref):
    t = pl.program_id(0)
    arrived = arr_ref[...]
    g = g_ref[...].reshape(COLS, WID)
    out = dot(arrived, w_ref[...], TN).astype(BF16)
    out_ref[...] = out.reshape(FR_DEV, 1, TILE, WID)
    term = dot(arrived, g)

    @pl.when(t == 0)
    def _():
        acc_ref[...] = term

    @pl.when(t > 0)
    def _():
        acc_ref[...] += term

    @pl.when(t == NTILE - 1)
    def _():
        full = dot(placer_of(perm_ref, True), acc_ref[...].astype(BF16))
        for c in range(HL):
            l_ref[c] = full[c * BLK : (c + 1) * BLK, c * BLK : (c + 1) * BLK].astype(BF16)


def project(perm, w, arrived, g4):
    return pl.pallas_call(
        project_kernel,
        grid=(NTILE,),
        in_specs=[smem(), whole((WID, WID)), col_spec(), tile_spec(FR_DEV)],
        out_specs=[tile_spec(FR_DEV), whole((HL, BLK, BLK))],
        out_shape=[
            jax.ShapeDtypeStruct((FR_DEV, NTILE, TILE, WID), BF16),
            jax.ShapeDtypeStruct((HL, BLK, BLK), BF16),
        ],
        scratch_shapes=[pltpu.VMEM((WID, WID), F32)],
        compiler_params=params(),
        cost_estimate=pl.CostEstimate(flops=10**9, bytes_accessed=6 * 10**6, transcendentals=0),
        name="project",
    )(perm, w, arrived, g4)


def tm_sum(x, norm):
    count = lax.axis_size("tm")

    def moved(y, to):
        return lax.ppermute(y, "tm", [(i, to(i)) for i in range(count)]).astype(F32)

    def along_x(by):
        return lambda i: (i // 8) * 8 + (i % 8 + 2 * by) % 8

    x = (x.astype(F32) + moved(x, lambda i: i ^ 1)).astype(BF16)
    one, two, three = moved(x, along_x(1)), moved(x, along_x(2)), moved(x, along_x(3))
    x = ((x.astype(F32) + two) + (one + three)).astype(BF16)
    x = x.astype(F32) + moved(x, lambda i: i ^ 8)
    return x * norm


def on_device(queries, keys, values, right_blocks, left_blocks, block_perm, reach, grad_out):
    rows, width = queries.shape
    count = lax.axis_size("tm")
    n_head = lax.axis_size("head")
    up = [(i, (i + 1) % count) for i in range(count)]
    down = [((i + 1) % count, i) for i in range(count)]
    shape4 = (FR_DEV, NTILE, TILE, width)
    half = (RADIUS, NTILE, TILE, width)
    q4, k4, v4, g4 = (x.reshape(shape4) for x in (queries, keys, values, grad_out))
    cut = RADIUS * NTILE * TILE
    klo = lax.ppermute(keys[rows - cut :], "tm", up).reshape(half)
    khi = lax.ppermute(keys[:cut], "tm", down).reshape(half)
    vlo = lax.ppermute(values[rows - cut :], "tm", up).reshape(half)
    vhi = lax.ppermute(values[:cut], "tm", down).reshape(half)

    w, rb, d_arrived = prep(block_perm, left_blocks, right_blocks, g4)

    def exchange(x):
        y = lax.all_to_all(
            x.reshape(n_head, width // n_head, rows), "head", split_axis=0, concat_axis=0, tiled=True
        )
        return y.reshape(width, rows)

    dmix = exchange(d_arrived)
    attn_t, probs, mixed = forward(reach, q4, k4, v4, klo, khi, vlo, vhi, rb)
    arrived = exchange(mixed)
    dq, dk, dv, lo, hi, right_term = backward(
        q4, k4, v4, klo, khi, vlo, vhi, rb, attn_t, probs, dmix
    )
    below = lax.ppermute(hi, "tm", up)
    above = lax.ppermute(lo, "tm", down)
    projected, left_term = project(block_perm, w, arrived, g4)
    dk, dv = add_halos(dk, dv, below, above)
    norm = float(rows * count) ** (-0.5)
    d_right = tm_sum(right_term, norm)
    d_left = tm_sum(left_term, norm)
    flat = (rows, width)
    return (
        projected.reshape(flat),
        dq.reshape(flat),
        dk.reshape(flat),
        dv.reshape(flat),
        d_right,
        d_left,
    )


def solution(mesh):
    in_specs = (
        P("tm", "head"),
        P("tm", "head"),
        P("tm", "head"),
        P("head", None, None),
        P("head", None, None),
        P(),
        P(),
        P("tm", "head"),
    )
    out_specs = (
        P("tm", "head"),
        P("tm", "head"),
        P("tm", "head"),
        P("tm", "head"),
        P("head", None, None),
        P("head", None, None),
    )
    return jax.shard_map(
        on_device, mesh=mesh, in_specs=in_specs, out_specs=out_specs, check_vma=False
    )
```

```python
import functools

import jax
import jax.numpy as jnp
from jax import lax
from jax.experimental import pallas as pl
from jax.experimental.pallas import tpu as pltpu
from jax.sharding import PartitionSpec as P

NB = 24
BLK = 128
TILE = 128
RADIUS = 2
FR_DEV = 4
NTILE = 4
NF = 64
HL = 3
WID = HL * BLK
ROWS = FR_DEV * NTILE * TILE
COLS = FR_DEV * TILE
PIECE = 16
SCALE = BLK ** (-0.5)
LOG2E = 1.4426950408889634
NEG = -1e30
F32 = jnp.float32
BF16 = jnp.bfloat16
VMEM = 56 * 1024 * 1024

NN = (((1,), (0,)), ((), ()))
NT = (((1,), (1,)), ((), ()))
TN = (((0,), (0,)), ((), ()))


def dot(a, b, dims=NN):
    return lax.dot_general(a, b, dims, preferred_element_type=F32)


def params():
    return pltpu.CompilerParams(
        vmem_limit_bytes=VMEM, dimension_semantics=("arbitrary",)
    )


def placer_of(perm_ref, flip):
    shape = (WID, 1) if flip else (1, WID)
    col = lax.broadcasted_iota(jnp.int32, shape, 0 if flip else 1)
    block = lax.rem(col, NB)
    lane = lax.div(col, NB)
    source = jnp.zeros(shape, jnp.int32)
    for b in range(NB):
        source = jnp.where(block == b, perm_ref[b] * PIECE, source)
    source = source + lane
    row = lax.broadcasted_iota(jnp.int32, (WID, WID), 1 if flip else 0)
    return jnp.where(row == source, 1.0, 0.0).astype(BF16)


def block_diag(blocks):
    rows = []
    for c in range(HL):
        parts = [blocks[c] if d == c else jnp.zeros((BLK, BLK), BF16) for d in range(HL)]
        rows.append(jnp.concatenate(parts, axis=1))
    return jnp.concatenate(rows, axis=0)


def piece_order():
    col = lax.broadcasted_iota(jnp.int32, (1, WID), 1)
    s = lax.div(col, HL * PIECE)
    rest = col - s * (HL * PIECE)
    want = (rest // PIECE) * BLK + s * PIECE + rest % PIECE
    row = lax.broadcasted_iota(jnp.int32, (WID, WID), 0)
    return jnp.where(row == want, 1.0, 0.0).astype(BF16)


def piece_order_t():
    row = lax.broadcasted_iota(jnp.int32, (WID, 1), 0)
    s = lax.div(row, HL * PIECE)
    rest = row - s * (HL * PIECE)
    want = (rest // PIECE) * BLK + s * PIECE + rest % PIECE
    col = lax.broadcasted_iota(jnp.int32, (WID, WID), 1)
    return jnp.where(col == want, 1.0, 0.0).astype(BF16)


def eye(n):
    row = lax.broadcasted_iota(jnp.int32, (n, n), 0)
    col = lax.broadcasted_iota(jnp.int32, (n, n), 1)
    return jnp.where(row == col, 1.0, 0.0).astype(BF16)


def turned(x):
    return dot(eye(x.shape[1]), x, NT).astype(BF16)


def gate(x, *after):
    return pl.pallas_call(
        lambda *refs: None,
        in_specs=[pl.BlockSpec(memory_space=pl.ANY)] * (1 + len(after)),
        out_specs=pl.BlockSpec(memory_space=pl.ANY),
        out_shape=jax.ShapeDtypeStruct(x.shape, x.dtype),
        input_output_aliases={0: 0},
        compiler_params=pltpu.CompilerParams(vmem_limit_bytes=VMEM),
        name="gate",
    )(x, *after)


def whole(shape):
    return pl.BlockSpec(shape, lambda t: (0,) * len(shape))


def smem():
    return pl.BlockSpec(memory_space=pltpu.SMEM)


def tile_spec(frames, first=0):
    return pl.BlockSpec((frames, 1, TILE, WID), lambda t: (0, t + first, 0, 0))


def pair_spec():
    return pl.BlockSpec((2, RADIUS, 1, TILE, WID), lambda t: (0, 0, t, 0, 0))


def col_spec(first=0):
    return pl.BlockSpec((WID, COLS), lambda t: (0, t + first))


SPAN = 6
HALO = (2, RADIUS, NTILE, TILE, WID)
OUT4 = (FR_DEV, NTILE, TILE, WID)


def prep_kernel(perm_ref, left_ref, right_ref, g_ref, w_ref, rb_ref, rbt_ref, da_ref):
    @pl.when(pl.program_id(0) == 0)
    def _():
        w_ref[...] = dot(placer_of(perm_ref, False), block_diag(left_ref[...])).astype(BF16)
        rb = dot(block_diag(right_ref[...]), piece_order()).astype(BF16)
        rb_ref[...] = rb
        rbt_ref[...] = turned(rb)

    g = g_ref[...].reshape(COLS, WID)
    da_ref[...] = dot(w_ref[...], g, NT).astype(BF16)


def prep(perm, left, right, g4):
    square = jax.ShapeDtypeStruct((WID, WID), BF16)
    return pl.pallas_call(
        prep_kernel,
        grid=(NTILE,),
        in_specs=[smem(), whole((HL, BLK, BLK)), whole((HL, BLK, BLK)), tile_spec(FR_DEV)],
        out_specs=[whole((WID, WID))] * 3 + [col_spec()],
        out_shape=[square] * 3 + [jax.ShapeDtypeStruct((WID, ROWS), BF16)],
        compiler_params=params(),
        cost_estimate=pl.CostEstimate(flops=10**9, bytes_accessed=4 * 10**6, transcendentals=0),
        name="prep",
    )(perm, left, right, g4)


def ext_rows(lo, own, hi, which, h):
    cols = slice(h * BLK, (h + 1) * BLK)
    parts = [lo[which][e, 0, :, cols] for e in range(RADIUS)]
    parts += [own[e, 0, :, cols] for e in range(FR_DEV)]
    parts += [hi[which][e, 0, :, cols] for e in range(RADIUS)]
    return jnp.concatenate(parts, axis=0)


def ext_span(pair):
    return slice(2 * pair * TILE, (2 * pair + SPAN) * TILE)


UNITS = [(h, pair) for h in range(HL) for pair in range(2)]


def forward_kernel(
    reach_ref, q_ref, k_ref, v_ref, klo, khi, vlo, vhi, rbt_ref, at_ref, p_ref, inv_ref, mix_ref
):
    lo, hi = (klo, vlo), (khi, vhi)
    base = lax.axis_index("tm") * FR_DEV
    head0 = lax.axis_index("head") * HL
    ones = jnp.ones((16, (FR_DEV + 2 * RADIUS) * TILE), BF16)
    vts = {}

    def scores(h, pair):
        cols = slice(h * BLK, (h + 1) * BLK)
        q = q_ref[2 * pair : 2 * pair + 2, 0, :, cols].reshape(2 * TILE, BLK)
        return dot(ext_rows(lo, k_ref, hi, 0, h)[ext_span(pair)], q, NT)

    s_next = scores(*UNITS[0])
    for index, (h, pair) in enumerate(UNITS):
        s = s_next
        if index + 1 < len(UNITS):
            s_next = scores(*UNITS[index + 1])
        if pair == 0:
            vts[h] = jnp.concatenate([ext_rows(lo, v_ref, hi, 1, h).T, ones], axis=0)
        reach = reach_ref[head0 + h]
        f0 = 2 * pair
        halves = []
        for a in range(2):
            parts, rows = [], []
            for j in range(5):
                frame = base + f0 + a + j - RADIUS
                ok = (abs(j - RADIUS) <= reach) & (frame >= 0) & (frame < NF)
                e = a + j
                x = s[e * TILE : (e + 1) * TILE, a * TILE : (a + 1) * TILE]
                bias = jnp.where(ok, 0.0, NEG)
                parts.append((x, bias))
                rows.append(jnp.max(x, axis=0, keepdims=True) * (SCALE * LOG2E) + bias)
            top = functools.reduce(jnp.maximum, rows)
            x = [jnp.exp2(x * (SCALE * LOG2E) + (bias - top)).astype(BF16) for x, bias in parts]
            zero = [jnp.zeros((TILE, TILE), BF16)]
            halves.append(jnp.concatenate(x + zero if a == 0 else zero + x, axis=0))
        p = jnp.concatenate(halves, axis=1)
        p_ref[0, h, pair] = p
        out = dot(vts[h][:, ext_span(pair)], p)
        inv = 1.0 / out[BLK : BLK + 1]
        lanes = slice(f0 * TILE, (f0 + 2) * TILE)
        inv_ref[0, h : h + 1, lanes] = inv
        at_ref[h * BLK : (h + 1) * BLK, lanes] = (out[:BLK] * inv).astype(BF16)
    mix_ref[...] = dot(rbt_ref[...], at_ref[...]).astype(BF16)


def p_spec():
    return pl.BlockSpec((1, HL, 2, SPAN * TILE, 2 * TILE), lambda t: (t, 0, 0, 0, 0))


def inv_spec():
    return pl.BlockSpec((1, 8, COLS), lambda t: (t, 0, 0))


def forward(reach, q4, k4, v4, halos, rbt):
    cols = jax.ShapeDtypeStruct((WID, ROWS), BF16)
    return pl.pallas_call(
        forward_kernel,
        grid=(NTILE,),
        in_specs=[smem()]
        + [tile_spec(FR_DEV)] * 3
        + [tile_spec(RADIUS)] * 4
        + [whole((WID, WID))],
        out_specs=[col_spec(), p_spec(), inv_spec(), col_spec()],
        out_shape=[
            cols,
            jax.ShapeDtypeStruct((NTILE, HL, 2, SPAN * TILE, 2 * TILE), BF16),
            jax.ShapeDtypeStruct((NTILE, 8, COLS), F32),
            cols,
        ],
        compiler_params=params(),
        cost_estimate=pl.CostEstimate(
            flops=6 * 10**9, bytes_accessed=20 * 10**6, transcendentals=4 * 10**6
        ),
        name="forward",
    )(reach, q4, k4, v4, *halos, rbt)


def backward_kernel(
    q_ref, k_ref, v_ref, klo, khi, vlo, vhi, rb_ref, at_ref, p_ref, inv_ref, dm_ref,
    dq_ref, dk_ref, dv_ref, lo_ref, hi_ref, r_ref, acc_ref,
):
    lo, hi = (klo, vlo), (khi, vhi)
    t = pl.program_id(0)
    term = dot(at_ref[...], dm_ref[...], NT)

    @pl.when(t == 0)
    def _():
        acc_ref[...] = term

    @pl.when(t > 0)
    def _():
        acc_ref[...] += term

    dat_all = dot(rb_ref[...], dm_ref[...])

    def start(h, pair):
        cols = slice(h * BLK, (h + 1) * BLK)
        lanes = slice(2 * pair * TILE, (2 * pair + 2) * TILE)
        d_t = (dat_all[cols, lanes] * inv_ref[0, h : h + 1, lanes]).astype(BF16)
        delta = jnp.sum(d_t.astype(F32) * at_ref[cols, lanes].astype(F32), axis=0, keepdims=True)
        return d_t, delta, dot(ext_rows(lo, v_ref, hi, 1, h)[ext_span(pair)], d_t)

    coming = start(*UNITS[0])
    for h in range(HL):
        cols = slice(h * BLK, (h + 1) * BLK)
        k = ext_rows(lo, k_ref, hi, 0, h)
        dks, dvs = [], []
        for pair in range(2):
            d_t, delta, dp = coming
            index = 2 * h + pair + 1
            if index < len(UNITS):
                coming = start(*UNITS[index])
            f0 = 2 * pair
            q = q_ref[f0 : f0 + 2, 0, :, cols].reshape(2 * TILE, BLK)
            p = p_ref[0, h, pair]
            dvs.append(dot(p, d_t, NT))
            grads = (p.astype(F32) * (dp - delta)).astype(BF16)
            dks.append(dot(grads, q) * SCALE)
            dq = (dot(grads, k[ext_span(pair)], TN) * SCALE).astype(BF16)
            dq_ref[f0 : f0 + 2, 0, :, cols] = dq.reshape(2, TILE, BLK)
        for which, (low, high) in enumerate((dks, dvs)):
            own_ref = dk_ref if which == 0 else dv_ref
            for e in range(RADIUS):
                lo_ref[which, e, 0, :, cols] = low[e * TILE : (e + 1) * TILE].astype(BF16)
                hi_ref[which, e, 0, :, cols] = high[(e + 4) * TILE : (e + 5) * TILE].astype(BF16)
            for e in range(FR_DEV):
                own = low[(e + 2) * TILE : (e + 3) * TILE] + high[e * TILE : (e + 1) * TILE]
                own_ref[e, 0, :, cols] = own.astype(BF16)

    @pl.when(t == NTILE - 1)
    def _():
        full = dot(acc_ref[...].astype(BF16), piece_order_t())
        for b in range(HL):
            r_ref[b] = full[b * BLK : (b + 1) * BLK, b * BLK : (b + 1) * BLK].astype(BF16)


def backward(q4, k4, v4, halos, rb, attn_t, probs, inv, dmix):
    out4 = jax.ShapeDtypeStruct(OUT4, BF16)
    halo = jax.ShapeDtypeStruct(HALO, BF16)
    end = (HL, BLK, BLK)
    return pl.pallas_call(
        backward_kernel,
        grid=(NTILE,),
        in_specs=[tile_spec(FR_DEV)] * 3
        + [tile_spec(RADIUS)] * 4
        + [whole((WID, WID)), col_spec(), p_spec(), inv_spec(), col_spec()],
        out_specs=[tile_spec(FR_DEV)] * 3 + [pair_spec()] * 2 + [whole(end)],
        out_shape=[out4] * 3 + [halo] * 2 + [jax.ShapeDtypeStruct(end, BF16)],
        scratch_shapes=[pltpu.VMEM((WID, WID), F32)],
        compiler_params=params(),
        cost_estimate=pl.CostEstimate(
            flops=12 * 10**9, bytes_accessed=30 * 10**6, transcendentals=0
        ),
        name="backward",
    )(q4, k4, v4, *halos, rb, attn_t, probs, inv, dmix)


def add_kernel(dk_ref, dv_ref, below_ref, above_ref, ok_ref, ov_ref):
    for which, (own, out) in enumerate(((dk_ref, ok_ref), (dv_ref, ov_ref))):
        for e in range(RADIUS):
            out[e] = (own[e].astype(F32) + below_ref[which, e].astype(F32)).astype(BF16)
            up = own[RADIUS + e].astype(F32) + above_ref[which, e].astype(F32)
            out[RADIUS + e] = up.astype(BF16)


def add_halos(dk, dv, below, above):
    return pl.pallas_call(
        add_kernel,
        grid=(NTILE,),
        in_specs=[tile_spec(FR_DEV)] * 2 + [pair_spec()] * 2,
        out_specs=[tile_spec(FR_DEV)] * 2,
        out_shape=[jax.ShapeDtypeStruct(OUT4, BF16)] * 2,
        compiler_params=params(),
        cost_estimate=pl.CostEstimate(flops=10**6, bytes_accessed=10 * 10**6, transcendentals=0),
        name="add_halos",
    )(dk, dv, below, above)


def left_kernel(perm_ref, arr_ref, g_ref, l_ref, acc_ref):
    t = pl.program_id(0)
    term = dot(arr_ref[...], g_ref[...].reshape(COLS, WID))

    @pl.when(t == 0)
    def _():
        acc_ref[...] = term

    @pl.when(t > 0)
    def _():
        acc_ref[...] += term

    @pl.when(t == NTILE - 1)
    def _():
        full = dot(placer_of(perm_ref, True), acc_ref[...].astype(BF16))
        for c in range(HL):
            l_ref[c] = full[c * BLK : (c + 1) * BLK, c * BLK : (c + 1) * BLK].astype(BF16)


def left_sum(perm, arrived, g4):
    return pl.pallas_call(
        left_kernel,
        grid=(NTILE,),
        in_specs=[smem(), col_spec(), tile_spec(FR_DEV)],
        out_specs=whole((HL, BLK, BLK)),
        out_shape=jax.ShapeDtypeStruct((HL, BLK, BLK), BF16),
        scratch_shapes=[pltpu.VMEM((WID, WID), F32)],
        compiler_params=params(),
        cost_estimate=pl.CostEstimate(flops=10**9, bytes_accessed=4 * 10**6, transcendentals=0),
        name="left_sum",
    )(perm, arrived, g4)


def project_kernel(w_ref, arr_ref, _, out_ref):
    for n in range(2):
        part = arr_ref[:, n * 2 * TILE : (n + 1) * 2 * TILE]
        out = dot(part, w_ref[...], TN).astype(BF16)
        out_ref[2 * n : 2 * n + 2] = out.reshape(2, 1, TILE, WID)


def project(w, arrived, after):
    return pl.pallas_call(
        project_kernel,
        grid=(NTILE,),
        in_specs=[whole((WID, WID)), col_spec(), pl.BlockSpec(memory_space=pl.ANY)],
        out_specs=tile_spec(FR_DEV),
        out_shape=jax.ShapeDtypeStruct(OUT4, BF16),
        compiler_params=params(),
        cost_estimate=pl.CostEstimate(flops=10**9, bytes_accessed=4 * 10**6, transcendentals=0),
        name="project",
    )(w, arrived, after)


def tm_sums(right, left, norm, projected, dk):
    count = lax.axis_size("tm")
    first = lax.axis_index("tm") % 2 == 0

    def moved(y, to):
        return lax.ppermute(y, "tm", [(i, to(i)) for i in range(count)])

    def along_x(by):
        return lambda i: (i // 8) * 8 + (i % 8 + 2 * by) % 8

    x = jnp.where(first, right, left).astype(F32)
    x = (x + moved(jnp.where(first, left, right), lambda i: i ^ 1).astype(F32)).astype(BF16)
    x = (x.astype(F32) + moved(x, lambda i: i ^ 8).astype(F32)).astype(BF16)
    x = gate(x, projected)
    one, two, three = (moved(x, along_x(by)).astype(F32) for by in (1, 2, 3))
    x = ((x.astype(F32) + two) + (one + three)).astype(BF16)
    x = gate(x, dk)
    other = moved(x, lambda i: i ^ 1).astype(F32) * norm
    x = x.astype(F32) * norm
    return jnp.where(first, x, other), jnp.where(first, other, x)


def on_device(queries, keys, values, right_blocks, left_blocks, block_perm, reach, grad_out):
    rows, width = queries.shape
    count = lax.axis_size("tm")
    n_head = lax.axis_size("head")
    up = [(i, (i + 1) % count) for i in range(count)]
    down = [((i + 1) % count, i) for i in range(count)]
    shape4 = (FR_DEV, NTILE, TILE, width)
    q4, k4, v4, g4 = (x.reshape(shape4) for x in (queries, keys, values, grad_out))
    half = (RADIUS, NTILE, TILE, width)
    cut = RADIUS * NTILE * TILE
    halos = [
        lax.ppermute(keys[rows - cut :], "tm", up).reshape(half),
        lax.ppermute(keys[:cut], "tm", down).reshape(half),
        lax.ppermute(values[rows - cut :], "tm", up).reshape(half),
        lax.ppermute(values[:cut], "tm", down).reshape(half),
    ]
    w, rb, rbt, d_arrived = prep(block_perm, left_blocks, right_blocks, g4)

    def exchange(x):
        y = lax.all_to_all(
            x.reshape(n_head, width // n_head, rows), "head", split_axis=0, concat_axis=0, tiled=True
        )
        return y.reshape(width, rows)

    dmix = exchange(d_arrived)
    attn_t, probs, inv, mixed = forward(reach, q4, k4, v4, halos, rbt)
    arrived = exchange(mixed)
    dq, dk, dv, lo, hi, right_term = backward(q4, k4, v4, halos, rb, attn_t, probs, inv, dmix)
    below = lax.ppermute(hi, "tm", up)
    above = lax.ppermute(lo, "tm", down)
    left_term = left_sum(block_perm, arrived, g4)
    projected = project(w, arrived, left_term)
    dk, dv = add_halos(dk, dv, below, above)
    norm = float(rows * count) ** (-0.5)
    d_right, d_left = tm_sums(right_term, left_term, norm, projected, dk)
    flat = (rows, width)
    return (
        projected.reshape(flat),
        dq.reshape(flat),
        dk.reshape(flat),
        dv.reshape(flat),
        d_right,
        d_left,
    )


def solution(mesh):
    in_specs = (
        P("tm", "head"),
        P("tm", "head"),
        P("tm", "head"),
        P("head", None, None),
        P("head", None, None),
        P(),
        P(),
        P("tm", "head"),
    )
    out_specs = (
        P("tm", "head"),
        P("tm", "head"),
        P("tm", "head"),
        P("tm", "head"),
        P("head", None, None),
        P("head", None, None),
    )
    return jax.shard_map(
        on_device, mesh=mesh, in_specs=in_specs, out_specs=out_specs, check_vma=False
    )
```

```python
import functools

import jax
import jax.numpy as jnp
from jax import lax
from jax.experimental import pallas as pl
from jax.experimental.pallas import tpu as pltpu
from jax.sharding import PartitionSpec as P

NB = 24
BLK = 128
TILE = 128
RADIUS = 2
FR_DEV = 4
NTILE = 4
NF = 64
HL = 3
WID = HL * BLK
ROWS = FR_DEV * NTILE * TILE
COLS = FR_DEV * TILE
PIECE = 16
SCALE = BLK ** (-0.5)
LOG2E = 1.4426950408889634
NEG = -1e30
F32 = jnp.float32
BF16 = jnp.bfloat16
VMEM = 56 * 1024 * 1024

NN = (((1,), (0,)), ((), ()))
NT = (((1,), (1,)), ((), ()))
TN = (((0,), (0,)), ((), ()))


def dot(a, b, dims=NN):
    return lax.dot_general(a, b, dims, preferred_element_type=F32)


def params(mib=56):
    return pltpu.CompilerParams(
        vmem_limit_bytes=mib * 1024 * 1024, dimension_semantics=("arbitrary",)
    )


def placer_of(perm_ref, flip):
    shape = (WID, 1) if flip else (1, WID)
    col = lax.broadcasted_iota(jnp.int32, shape, 0 if flip else 1)
    block = lax.rem(col, NB)
    lane = lax.div(col, NB)
    source = jnp.zeros(shape, jnp.int32)
    for b in range(NB):
        source = jnp.where(block == b, perm_ref[b] * PIECE, source)
    source = source + lane
    row = lax.broadcasted_iota(jnp.int32, (WID, WID), 1 if flip else 0)
    return jnp.where(row == source, 1.0, 0.0).astype(BF16)


def block_diag(blocks):
    rows = []
    for c in range(HL):
        parts = [blocks[c] if d == c else jnp.zeros((BLK, BLK), BF16) for d in range(HL)]
        rows.append(jnp.concatenate(parts, axis=1))
    return jnp.concatenate(rows, axis=0)


def piece_order():
    col = lax.broadcasted_iota(jnp.int32, (1, WID), 1)
    s = lax.div(col, HL * PIECE)
    rest = col - s * (HL * PIECE)
    want = (rest // PIECE) * BLK + s * PIECE + rest % PIECE
    row = lax.broadcasted_iota(jnp.int32, (WID, WID), 0)
    return jnp.where(row == want, 1.0, 0.0).astype(BF16)


def piece_order_t():
    row = lax.broadcasted_iota(jnp.int32, (WID, 1), 0)
    s = lax.div(row, HL * PIECE)
    rest = row - s * (HL * PIECE)
    want = (rest // PIECE) * BLK + s * PIECE + rest % PIECE
    col = lax.broadcasted_iota(jnp.int32, (WID, WID), 1)
    return jnp.where(col == want, 1.0, 0.0).astype(BF16)


def eye(n):
    row = lax.broadcasted_iota(jnp.int32, (n, n), 0)
    col = lax.broadcasted_iota(jnp.int32, (n, n), 1)
    return jnp.where(row == col, 1.0, 0.0).astype(BF16)


def turned(x):
    return dot(eye(x.shape[1]), x, NT).astype(BF16)


def gate(x, *after):
    return pl.pallas_call(
        lambda *refs: None,
        in_specs=[pl.BlockSpec(memory_space=pl.ANY)] * (1 + len(after)),
        out_specs=pl.BlockSpec(memory_space=pl.ANY),
        out_shape=jax.ShapeDtypeStruct(x.shape, x.dtype),
        input_output_aliases={0: 0},
        compiler_params=pltpu.CompilerParams(vmem_limit_bytes=VMEM),
        name="gate",
    )(x, *after)


def whole(shape):
    return pl.BlockSpec(shape, lambda t: (0,) * len(shape))


def smem():
    return pl.BlockSpec(memory_space=pltpu.SMEM)


def tile_spec(frames, first=0):
    return pl.BlockSpec((frames, 1, TILE, WID), lambda t: (0, t + first, 0, 0))


def pair_spec():
    return pl.BlockSpec((2, RADIUS, 1, TILE, WID), lambda t: (0, 0, t, 0, 0))


def col_spec(first=0):
    return pl.BlockSpec((WID, COLS), lambda t: (0, t + first))


SPAN = 6
HALO = (2, RADIUS, NTILE, TILE, WID)
OUT4 = (FR_DEV, NTILE, TILE, WID)


def prep_kernel(perm_ref, left_ref, g_ref, w_ref, da_ref):
    @pl.when(pl.program_id(0) == 0)
    def _():
        w_ref[...] = dot(placer_of(perm_ref, False), block_diag(left_ref[...])).astype(BF16)

    da_ref[...] = dot(w_ref[...], g_ref[...].reshape(COLS, WID), NT).astype(BF16)


def prep(perm, left, g4):
    return pl.pallas_call(
        prep_kernel,
        grid=(NTILE,),
        in_specs=[smem(), whole((HL, BLK, BLK)), tile_spec(FR_DEV)],
        out_specs=[whole((WID, WID)), col_spec()],
        out_shape=[
            jax.ShapeDtypeStruct((WID, WID), BF16),
            jax.ShapeDtypeStruct((WID, ROWS), BF16),
        ],
        compiler_params=params(),
        cost_estimate=pl.CostEstimate(flops=10**9, bytes_accessed=4 * 10**6, transcendentals=0),
        name="prep",
    )(perm, left, g4)


def orders_kernel(perm_ref, right_ref, rb_ref, rbt_ref, back_ref):
    rb = dot(block_diag(right_ref[...]), piece_order()).astype(BF16)
    rb_ref[...] = rb
    rbt_ref[...] = turned(rb)
    back_ref[...] = placer_of(perm_ref, True)


def orders(perm, right):
    square = jax.ShapeDtypeStruct((WID, WID), BF16)
    return pl.pallas_call(
        orders_kernel,
        in_specs=[smem(), pl.BlockSpec(memory_space=pltpu.VMEM)],
        out_specs=[pl.BlockSpec(memory_space=pltpu.VMEM)] * 3,
        out_shape=[square] * 3,
        compiler_params=pltpu.CompilerParams(vmem_limit_bytes=VMEM),
        cost_estimate=pl.CostEstimate(flops=3 * 10**8, bytes_accessed=10**6, transcendentals=0),
        name="orders",
    )(perm, right)


def ext_rows(lo, own, hi, which, h):
    cols = slice(h * BLK, (h + 1) * BLK)
    parts = [lo[which][e, 0, :, cols] for e in range(RADIUS)]
    parts += [own[e, 0, :, cols] for e in range(FR_DEV)]
    parts += [hi[which][e, 0, :, cols] for e in range(RADIUS)]
    return jnp.concatenate(parts, axis=0)


def ext_span(pair):
    return slice(2 * pair * TILE, (2 * pair + SPAN) * TILE)


UNITS = [(h, pair) for h in range(HL) for pair in range(2)]


def forward_kernel(
    reach_ref, q_ref, k_ref, v_ref, klo, khi, vlo, vhi, rbt_ref, at_ref, p_ref, inv_ref, mix_ref
):
    lo, hi = (klo, vlo), (khi, vhi)
    base = lax.axis_index("tm") * FR_DEV
    head0 = lax.axis_index("head") * HL
    ones = jnp.ones((16, (FR_DEV + 2 * RADIUS) * TILE), BF16)
    vts = {}

    def scores(h, pair):
        cols = slice(h * BLK, (h + 1) * BLK)
        q = q_ref[2 * pair : 2 * pair + 2, 0, :, cols].reshape(2 * TILE, BLK)
        return dot(ext_rows(lo, k_ref, hi, 0, h)[ext_span(pair)], q, NT)

    s_next = scores(*UNITS[0])
    for index, (h, pair) in enumerate(UNITS):
        s = s_next
        if index + 1 < len(UNITS):
            s_next = scores(*UNITS[index + 1])
        if pair == 0:
            vts[h] = jnp.concatenate([ext_rows(lo, v_ref, hi, 1, h).T, ones], axis=0)
        reach = reach_ref[head0 + h]
        f0 = 2 * pair
        halves = []
        for a in range(2):
            parts, rows = [], []
            for j in range(5):
                frame = base + f0 + a + j - RADIUS
                ok = (abs(j - RADIUS) <= reach) & (frame >= 0) & (frame < NF)
                e = a + j
                x = s[e * TILE : (e + 1) * TILE, a * TILE : (a + 1) * TILE]
                bias = jnp.where(ok, 0.0, NEG)
                parts.append((x, bias))
                rows.append(jnp.max(x, axis=0, keepdims=True) * (SCALE * LOG2E) + bias)
            top = functools.reduce(jnp.maximum, rows)
            x = [jnp.exp2(x * (SCALE * LOG2E) + (bias - top)).astype(BF16) for x, bias in parts]
            zero = [jnp.zeros((TILE, TILE), BF16)]
            halves.append(jnp.concatenate(x + zero if a == 0 else zero + x, axis=0))
        p = jnp.concatenate(halves, axis=1)
        p_ref[0, h, pair] = p
        out = dot(vts[h][:, ext_span(pair)], p)
        inv = 1.0 / out[BLK : BLK + 1]
        lanes = slice(f0 * TILE, (f0 + 2) * TILE)
        inv_ref[0, h : h + 1, lanes] = inv
        at_ref[h * BLK : (h + 1) * BLK, lanes] = (out[:BLK] * inv).astype(BF16)
    mix_ref[...] = dot(rbt_ref[...], at_ref[...]).astype(BF16)


def p_spec():
    return pl.BlockSpec((1, HL, 2, SPAN * TILE, 2 * TILE), lambda t: (t, 0, 0, 0, 0))


def inv_spec():
    return pl.BlockSpec((1, 8, COLS), lambda t: (t, 0, 0))


def forward(reach, q4, k4, v4, halos, rbt):
    cols = jax.ShapeDtypeStruct((WID, ROWS), BF16)
    return pl.pallas_call(
        forward_kernel,
        grid=(NTILE,),
        in_specs=[smem()]
        + [tile_spec(FR_DEV)] * 3
        + [tile_spec(RADIUS)] * 4
        + [whole((WID, WID))],
        out_specs=[col_spec(), p_spec(), inv_spec(), col_spec()],
        out_shape=[
            cols,
            jax.ShapeDtypeStruct((NTILE, HL, 2, SPAN * TILE, 2 * TILE), BF16),
            jax.ShapeDtypeStruct((NTILE, 8, COLS), F32),
            cols,
        ],
        compiler_params=params(),
        cost_estimate=pl.CostEstimate(
            flops=6 * 10**9, bytes_accessed=20 * 10**6, transcendentals=4 * 10**6
        ),
        name="forward",
    )(reach, q4, k4, v4, *halos, rbt)


def backward_kernel(
    q_ref, k_ref, v_ref, klo, khi, vlo, vhi, rb_ref, at_ref, p_ref, inv_ref, dm_ref,
    dq_ref, dk_ref, dv_ref, lo_ref, hi_ref, r_ref, acc_ref,
):
    lo, hi = (klo, vlo), (khi, vhi)
    t = pl.program_id(0)
    term = dot(at_ref[...], dm_ref[...], NT)

    @pl.when(t == 0)
    def _():
        acc_ref[...] = term

    @pl.when(t > 0)
    def _():
        acc_ref[...] += term

    dat_all = dot(rb_ref[...], dm_ref[...])

    def start(h, pair):
        cols = slice(h * BLK, (h + 1) * BLK)
        lanes = slice(2 * pair * TILE, (2 * pair + 2) * TILE)
        d_t = (dat_all[cols, lanes] * inv_ref[0, h : h + 1, lanes]).astype(BF16)
        delta = jnp.sum(d_t.astype(F32) * at_ref[cols, lanes].astype(F32), axis=0, keepdims=True)
        return d_t, delta, dot(ext_rows(lo, v_ref, hi, 1, h)[ext_span(pair)], d_t)

    coming = start(*UNITS[0])
    for h in range(HL):
        cols = slice(h * BLK, (h + 1) * BLK)
        k = ext_rows(lo, k_ref, hi, 0, h)
        dks, dvs = [], []
        for pair in range(2):
            d_t, delta, dp = coming
            index = 2 * h + pair + 1
            if index < len(UNITS):
                coming = start(*UNITS[index])
            f0 = 2 * pair
            q = q_ref[f0 : f0 + 2, 0, :, cols].reshape(2 * TILE, BLK)
            p = p_ref[0, h, pair]
            dvs.append(dot(p, d_t, NT))
            grads = (p.astype(F32) * (dp - delta)).astype(BF16)
            dks.append(dot(grads, q) * SCALE)
            dq = (dot(grads, k[ext_span(pair)], TN) * SCALE).astype(BF16)
            dq_ref[f0 : f0 + 2, 0, :, cols] = dq.reshape(2, TILE, BLK)
        for which, (low, high) in enumerate((dks, dvs)):
            own_ref = dk_ref if which == 0 else dv_ref
            for e in range(RADIUS):
                lo_ref[which, e, 0, :, cols] = low[e * TILE : (e + 1) * TILE].astype(BF16)
                hi_ref[which, e, 0, :, cols] = high[(e + 4) * TILE : (e + 5) * TILE].astype(BF16)
            for e in range(FR_DEV):
                own = low[(e + 2) * TILE : (e + 3) * TILE] + high[e * TILE : (e + 1) * TILE]
                own_ref[e, 0, :, cols] = own.astype(BF16)

    @pl.when(t == NTILE - 1)
    def _():
        full = dot(acc_ref[...].astype(BF16), piece_order_t())
        for b in range(HL):
            r_ref[b] = full[b * BLK : (b + 1) * BLK, b * BLK : (b + 1) * BLK].astype(BF16)


def backward(q4, k4, v4, halos, rb, attn_t, probs, inv, dmix):
    out4 = jax.ShapeDtypeStruct(OUT4, BF16)
    halo = jax.ShapeDtypeStruct(HALO, BF16)
    end = (HL, BLK, BLK)
    return pl.pallas_call(
        backward_kernel,
        grid=(NTILE,),
        in_specs=[tile_spec(FR_DEV)] * 3
        + [tile_spec(RADIUS)] * 4
        + [whole((WID, WID)), col_spec(), p_spec(), inv_spec(), col_spec()],
        out_specs=[tile_spec(FR_DEV)] * 3 + [pair_spec()] * 2 + [whole(end)],
        out_shape=[out4] * 3 + [halo] * 2 + [jax.ShapeDtypeStruct(end, BF16)],
        scratch_shapes=[pltpu.VMEM((WID, WID), F32)],
        compiler_params=params(),
        cost_estimate=pl.CostEstimate(
            flops=12 * 10**9, bytes_accessed=30 * 10**6, transcendentals=0
        ),
        name="backward",
    )(q4, k4, v4, *halos, rb, attn_t, probs, inv, dmix)


def add_kernel(dk_ref, dv_ref, below_ref, above_ref, ok_ref, ov_ref):
    for which, (own, out) in enumerate(((dk_ref, ok_ref), (dv_ref, ov_ref))):
        for e in range(RADIUS):
            out[e] = (own[e].astype(F32) + below_ref[which, e].astype(F32)).astype(BF16)
            up = own[RADIUS + e].astype(F32) + above_ref[which, e].astype(F32)
            out[RADIUS + e] = up.astype(BF16)


def add_halos(dk, dv, below, above):
    return pl.pallas_call(
        add_kernel,
        grid=(NTILE,),
        in_specs=[tile_spec(FR_DEV)] * 2 + [pair_spec()] * 2,
        out_specs=[tile_spec(FR_DEV)] * 2,
        out_shape=[jax.ShapeDtypeStruct(OUT4, BF16)] * 2,
        compiler_params=params(16),
        cost_estimate=pl.CostEstimate(flops=10**6, bytes_accessed=10 * 10**6, transcendentals=0),
        name="add_halos",
    )(dk, dv, below, above)


def left_kernel(back_ref, arr_ref, g_ref, l_ref, acc_ref):
    t = pl.program_id(0)
    term = dot(arr_ref[...], g_ref[...].reshape(COLS, WID))

    @pl.when(t == 0)
    def _():
        acc_ref[...] = term

    @pl.when(t > 0)
    def _():
        acc_ref[...] += term

    @pl.when(t == NTILE - 1)
    def _():
        full = dot(back_ref[...], acc_ref[...].astype(BF16))
        for c in range(HL):
            l_ref[c] = full[c * BLK : (c + 1) * BLK, c * BLK : (c + 1) * BLK].astype(BF16)


def left_sum(back, arrived, g4):
    return pl.pallas_call(
        left_kernel,
        grid=(NTILE,),
        in_specs=[whole((WID, WID)), col_spec(), tile_spec(FR_DEV)],
        out_specs=whole((HL, BLK, BLK)),
        out_shape=jax.ShapeDtypeStruct((HL, BLK, BLK), BF16),
        scratch_shapes=[pltpu.VMEM((WID, WID), F32)],
        compiler_params=params(16),
        cost_estimate=pl.CostEstimate(flops=10**9, bytes_accessed=4 * 10**6, transcendentals=0),
        name="left_sum",
    )(back, arrived, g4)


def project_kernel(w_ref, arr_ref, _, out_ref):
    for n in range(2):
        part = arr_ref[:, n * 2 * TILE : (n + 1) * 2 * TILE]
        out = dot(part, w_ref[...], TN).astype(BF16)
        out_ref[2 * n : 2 * n + 2] = out.reshape(2, 1, TILE, WID)


def project(w, arrived, after):
    return pl.pallas_call(
        project_kernel,
        grid=(NTILE,),
        in_specs=[whole((WID, WID)), col_spec(), pl.BlockSpec(memory_space=pl.ANY)],
        out_specs=tile_spec(FR_DEV),
        out_shape=jax.ShapeDtypeStruct(OUT4, BF16),
        compiler_params=params(16),
        cost_estimate=pl.CostEstimate(flops=10**9, bytes_accessed=4 * 10**6, transcendentals=0),
        name="project",
    )(w, arrived, after)


def tm_sums(right, left, norm, projected, dk):
    count = lax.axis_size("tm")
    first = lax.axis_index("tm") % 2 == 0

    def moved(y, to):
        return lax.ppermute(y, "tm", [(i, to(i)) for i in range(count)])

    def along_x(by):
        return lambda i: (i // 8) * 8 + (i % 8 + 2 * by) % 8

    x = jnp.where(first, right, left).astype(F32)
    x = (x + moved(jnp.where(first, left, right), lambda i: i ^ 1).astype(F32)).astype(BF16)
    one, two, three = (moved(x, along_x(by)).astype(F32) for by in (1, 2, 3))
    x = ((x.astype(F32) + two) + (one + three)).astype(BF16)
    x = gate(x, projected)
    far = gate(moved(x, lambda i: i ^ 8), dk)
    x = (x.astype(F32) + far.astype(F32)).astype(BF16)
    other = moved(x, lambda i: i ^ 1).astype(F32) * norm
    x = x.astype(F32) * norm
    return jnp.where(first, x, other), jnp.where(first, other, x)


def on_device(queries, keys, values, right_blocks, left_blocks, block_perm, reach, grad_out):
    rows, width = queries.shape
    count = lax.axis_size("tm")
    n_head = lax.axis_size("head")
    up = [(i, (i + 1) % count) for i in range(count)]
    down = [((i + 1) % count, i) for i in range(count)]
    shape4 = (FR_DEV, NTILE, TILE, width)
    q4, k4, v4, g4 = (x.reshape(shape4) for x in (queries, keys, values, grad_out))
    half = (RADIUS, NTILE, TILE, width)
    cut = RADIUS * NTILE * TILE
    halos = [
        lax.ppermute(keys[rows - cut :], "tm", up).reshape(half),
        lax.ppermute(keys[:cut], "tm", down).reshape(half),
        lax.ppermute(values[rows - cut :], "tm", up).reshape(half),
        lax.ppermute(values[:cut], "tm", down).reshape(half),
    ]
    w, d_arrived = prep(block_perm, left_blocks, g4)

    def exchange(x):
        y = lax.all_to_all(
            x.reshape(n_head, width // n_head, rows), "head", split_axis=0, concat_axis=0, tiled=True
        )
        return y.reshape(width, rows)

    dmix = exchange(d_arrived)
    rb, rbt, back = orders(block_perm, right_blocks)
    attn_t, probs, inv, mixed = forward(reach, q4, k4, v4, halos, rbt)
    arrived = exchange(mixed)
    dq, dk, dv, lo, hi, right_term = backward(q4, k4, v4, halos, rb, attn_t, probs, inv, dmix)
    below = lax.ppermute(hi, "tm", up)
    above = lax.ppermute(lo, "tm", down)
    left_term = left_sum(back, arrived, g4)
    projected = project(w, arrived, left_term)
    dk, dv = add_halos(dk, dv, below, above)
    norm = float(rows * count) ** (-0.5)
    d_right, d_left = tm_sums(right_term, left_term, norm, projected, dk)
    flat = (rows, width)
    return (
        projected.reshape(flat),
        dq.reshape(flat),
        dk.reshape(flat),
        dv.reshape(flat),
        d_right,
        d_left,
    )


def solution(mesh):
    in_specs = (
        P("tm", "head"),
        P("tm", "head"),
        P("tm", "head"),
        P("head", None, None),
        P("head", None, None),
        P(),
        P(),
        P("tm", "head"),
    )
    out_specs = (
        P("tm", "head"),
        P("tm", "head"),
        P("tm", "head"),
        P("tm", "head"),
        P("head", None, None),
        P("head", None, None),
    )
    return jax.shard_map(
        on_device, mesh=mesh, in_specs=in_specs, out_specs=out_specs, check_vma=False
    )
```

```python
import functools

import jax
import jax.numpy as jnp
from jax import lax
from jax.experimental import pallas as pl
from jax.experimental.pallas import tpu as pltpu
from jax.sharding import PartitionSpec as P

NB = 24
BLK = 128
TILE = 128
RADIUS = 2
FR_DEV = 4
NTILE = 4
NF = 64
HL = 3
WID = HL * BLK
ROWS = FR_DEV * NTILE * TILE
COLS = FR_DEV * TILE
PIECE = 16
SCALE = BLK ** (-0.5)
LOG2E = 1.4426950408889634
NEG = -1e30
F32 = jnp.float32
BF16 = jnp.bfloat16
VMEM = 56 * 1024 * 1024

NN = (((1,), (0,)), ((), ()))
NT = (((1,), (1,)), ((), ()))
TN = (((0,), (0,)), ((), ()))


def dot(a, b, dims=NN):
    return lax.dot_general(a, b, dims, preferred_element_type=F32)


def params(mib=56):
    return pltpu.CompilerParams(
        vmem_limit_bytes=mib * 1024 * 1024, dimension_semantics=("arbitrary",)
    )


def placer_of(perm_ref, flip):
    shape = (WID, 1) if flip else (1, WID)
    col = lax.broadcasted_iota(jnp.int32, shape, 0 if flip else 1)
    block = lax.rem(col, NB)
    lane = lax.div(col, NB)
    source = jnp.zeros(shape, jnp.int32)
    for b in range(NB):
        source = jnp.where(block == b, perm_ref[b] * PIECE, source)
    source = source + lane
    row = lax.broadcasted_iota(jnp.int32, (WID, WID), 1 if flip else 0)
    return jnp.where(row == source, 1.0, 0.0).astype(BF16)


def block_diag(blocks):
    rows = []
    for c in range(HL):
        parts = [blocks[c] if d == c else jnp.zeros((BLK, BLK), BF16) for d in range(HL)]
        rows.append(jnp.concatenate(parts, axis=1))
    return jnp.concatenate(rows, axis=0)


def piece_order():
    col = lax.broadcasted_iota(jnp.int32, (1, WID), 1)
    s = lax.div(col, HL * PIECE)
    rest = col - s * (HL * PIECE)
    want = (rest // PIECE) * BLK + s * PIECE + rest % PIECE
    row = lax.broadcasted_iota(jnp.int32, (WID, WID), 0)
    return jnp.where(row == want, 1.0, 0.0).astype(BF16)


def piece_order_t():
    row = lax.broadcasted_iota(jnp.int32, (WID, 1), 0)
    s = lax.div(row, HL * PIECE)
    rest = row - s * (HL * PIECE)
    want = (rest // PIECE) * BLK + s * PIECE + rest % PIECE
    col = lax.broadcasted_iota(jnp.int32, (WID, WID), 1)
    return jnp.where(col == want, 1.0, 0.0).astype(BF16)


def eye(n):
    row = lax.broadcasted_iota(jnp.int32, (n, n), 0)
    col = lax.broadcasted_iota(jnp.int32, (n, n), 1)
    return jnp.where(row == col, 1.0, 0.0).astype(BF16)


def turned(x):
    return dot(eye(x.shape[1]), x, NT).astype(BF16)


def gate(x, *after):
    return pl.pallas_call(
        lambda *refs: None,
        in_specs=[pl.BlockSpec(memory_space=pl.ANY)] * (1 + len(after)),
        out_specs=pl.BlockSpec(memory_space=pl.ANY),
        out_shape=jax.ShapeDtypeStruct(x.shape, x.dtype),
        input_output_aliases={0: 0},
        compiler_params=pltpu.CompilerParams(vmem_limit_bytes=VMEM),
        name="gate",
    )(x, *after)


def whole(shape):
    return pl.BlockSpec(shape, lambda t: (0,) * len(shape))


def smem():
    return pl.BlockSpec(memory_space=pltpu.SMEM)


def tile_spec(frames, first=0):
    return pl.BlockSpec((frames, 1, TILE, WID), lambda t: (0, t + first, 0, 0))


def pair_spec():
    return pl.BlockSpec((2, RADIUS, 1, TILE, WID), lambda t: (0, 0, t, 0, 0))


def col_spec(first=0):
    return pl.BlockSpec((WID, COLS), lambda t: (0, t + first))


SPAN = 6
HALO = (2, RADIUS, NTILE, TILE, WID)
OUT4 = (FR_DEV, NTILE, TILE, WID)


def prep_kernel(perm_ref, left_ref, g_ref, w_ref, da_ref):
    @pl.when(pl.program_id(0) == 0)
    def _():
        w_ref[...] = dot(placer_of(perm_ref, False), block_diag(left_ref[...])).astype(BF16)

    da_ref[...] = dot(w_ref[...], g_ref[...].reshape(COLS, WID), NT).astype(BF16)


def prep(perm, left, g4):
    return pl.pallas_call(
        prep_kernel,
        grid=(NTILE,),
        in_specs=[smem(), whole((HL, BLK, BLK)), tile_spec(FR_DEV)],
        out_specs=[whole((WID, WID)), col_spec()],
        out_shape=[
            jax.ShapeDtypeStruct((WID, WID), BF16),
            jax.ShapeDtypeStruct((WID, ROWS), BF16),
        ],
        compiler_params=params(),
        cost_estimate=pl.CostEstimate(flops=10**9, bytes_accessed=4 * 10**6, transcendentals=0),
        name="prep",
    )(perm, left, g4)


def orders_kernel(perm_ref, right_ref, rb_ref, rbt_ref, back_ref):
    rb = dot(block_diag(right_ref[...]), piece_order()).astype(BF16)
    rb_ref[...] = rb
    rbt_ref[...] = turned(rb)
    back_ref[...] = placer_of(perm_ref, True)


def orders(perm, right):
    square = jax.ShapeDtypeStruct((WID, WID), BF16)
    return pl.pallas_call(
        orders_kernel,
        in_specs=[smem(), pl.BlockSpec(memory_space=pltpu.VMEM)],
        out_specs=[pl.BlockSpec(memory_space=pltpu.VMEM)] * 3,
        out_shape=[square] * 3,
        compiler_params=pltpu.CompilerParams(vmem_limit_bytes=VMEM),
        cost_estimate=pl.CostEstimate(flops=3 * 10**8, bytes_accessed=10**6, transcendentals=0),
        name="orders",
    )(perm, right)


def ext_rows(lo, own, hi, which, h):
    cols = slice(h * BLK, (h + 1) * BLK)
    parts = [lo[which][e, 0, :, cols] for e in range(RADIUS)]
    parts += [own[e, 0, :, cols] for e in range(FR_DEV)]
    parts += [hi[which][e, 0, :, cols] for e in range(RADIUS)]
    return jnp.concatenate(parts, axis=0)


def ext_span(pair):
    return slice(2 * pair * TILE, (2 * pair + SPAN) * TILE)


UNITS = [(h, pair) for h in range(HL) for pair in range(2)]


def forward_kernel(
    reach_ref, q_ref, k_ref, v_ref, klo, khi, vlo, vhi, rbt_ref, at_ref, p_ref, inv_ref, mix_ref
):
    lo, hi = (klo, vlo), (khi, vhi)
    base = lax.axis_index("tm") * FR_DEV
    head0 = lax.axis_index("head") * HL
    ones = jnp.ones((16, (FR_DEV + 2 * RADIUS) * TILE), BF16)
    vts = {}

    def scores(h, pair):
        cols = slice(h * BLK, (h + 1) * BLK)
        q = q_ref[2 * pair : 2 * pair + 2, 0, :, cols].reshape(2 * TILE, BLK)
        return dot(ext_rows(lo, k_ref, hi, 0, h)[ext_span(pair)], q, NT)

    s_next = scores(*UNITS[0])
    for index, (h, pair) in enumerate(UNITS):
        s = s_next
        if index + 1 < len(UNITS):
            s_next = scores(*UNITS[index + 1])
        if pair == 0:
            vts[h] = jnp.concatenate([ext_rows(lo, v_ref, hi, 1, h).T, ones], axis=0)
        reach = reach_ref[head0 + h]
        f0 = 2 * pair
        halves = []
        for a in range(2):
            parts, rows = [], []
            for j in range(5):
                frame = base + f0 + a + j - RADIUS
                ok = (abs(j - RADIUS) <= reach) & (frame >= 0) & (frame < NF)
                e = a + j
                x = s[e * TILE : (e + 1) * TILE, a * TILE : (a + 1) * TILE]
                bias = jnp.where(ok, 0.0, NEG)
                parts.append((x, bias))
                rows.append(jnp.max(x, axis=0, keepdims=True) * (SCALE * LOG2E) + bias)
            top = functools.reduce(jnp.maximum, rows)
            x = [jnp.exp2(x * (SCALE * LOG2E) + (bias - top)).astype(BF16) for x, bias in parts]
            zero = [jnp.zeros((TILE, TILE), BF16)]
            halves.append(jnp.concatenate(x + zero if a == 0 else zero + x, axis=0))
        p = jnp.concatenate(halves, axis=1)
        p_ref[0, h, pair] = p
        out = dot(vts[h][:, ext_span(pair)], p)
        inv = 1.0 / out[BLK : BLK + 1]
        lanes = slice(f0 * TILE, (f0 + 2) * TILE)
        inv_ref[0, h : h + 1, lanes] = inv
        at_ref[h * BLK : (h + 1) * BLK, lanes] = (out[:BLK] * inv).astype(BF16)
    mix_ref[...] = dot(rbt_ref[...], at_ref[...]).astype(BF16)


def p_spec():
    return pl.BlockSpec((1, HL, 2, SPAN * TILE, 2 * TILE), lambda t: (t, 0, 0, 0, 0))


def inv_spec():
    return pl.BlockSpec((1, 8, COLS), lambda t: (t, 0, 0))


def forward(reach, q4, k4, v4, halos, rbt):
    cols = jax.ShapeDtypeStruct((WID, ROWS), BF16)
    return pl.pallas_call(
        forward_kernel,
        grid=(NTILE,),
        in_specs=[smem()]
        + [tile_spec(FR_DEV)] * 3
        + [tile_spec(RADIUS)] * 4
        + [whole((WID, WID))],
        out_specs=[col_spec(), p_spec(), inv_spec(), col_spec()],
        out_shape=[
            cols,
            jax.ShapeDtypeStruct((NTILE, HL, 2, SPAN * TILE, 2 * TILE), BF16),
            jax.ShapeDtypeStruct((NTILE, 8, COLS), F32),
            cols,
        ],
        compiler_params=params(),
        cost_estimate=pl.CostEstimate(
            flops=6 * 10**9, bytes_accessed=20 * 10**6, transcendentals=4 * 10**6
        ),
        name="forward",
    )(reach, q4, k4, v4, *halos, rbt)


def backward_kernel(
    q_ref, k_ref, v_ref, klo, khi, vlo, vhi, rb_ref, at_ref, p_ref, inv_ref, dm_ref,
    dq_ref, dk_ref, dv_ref, lo_ref, hi_ref, r_ref, acc_ref,
):
    lo, hi = (klo, vlo), (khi, vhi)
    t = pl.program_id(0)
    dat_all = dot(rb_ref[...], dm_ref[...])

    def start(h, pair):
        cols = slice(h * BLK, (h + 1) * BLK)
        lanes = slice(2 * pair * TILE, (2 * pair + 2) * TILE)
        d_t = (dat_all[cols, lanes] * inv_ref[0, h : h + 1, lanes]).astype(BF16)
        delta = jnp.sum(d_t.astype(F32) * at_ref[cols, lanes].astype(F32), axis=0, keepdims=True)
        return d_t, delta, dot(ext_rows(lo, v_ref, hi, 1, h)[ext_span(pair)], d_t)

    coming = start(*UNITS[0])
    for h in range(HL):
        cols = slice(h * BLK, (h + 1) * BLK)
        k = ext_rows(lo, k_ref, hi, 0, h)
        dks, dvs = [], []
        for pair in range(2):
            d_t, delta, dp = coming
            index = 2 * h + pair + 1
            if index < len(UNITS):
                coming = start(*UNITS[index])
            f0 = 2 * pair
            q = q_ref[f0 : f0 + 2, 0, :, cols].reshape(2 * TILE, BLK)
            p = p_ref[0, h, pair]
            dvs.append(dot(p, d_t, NT))
            grads = (p.astype(F32) * (dp - delta)).astype(BF16)
            dks.append(dot(grads, q) * SCALE)
            dq = (dot(grads, k[ext_span(pair)], TN) * SCALE).astype(BF16)
            dq_ref[f0 : f0 + 2, 0, :, cols] = dq.reshape(2, TILE, BLK)
        for which, (low, high) in enumerate((dks, dvs)):
            own_ref = dk_ref if which == 0 else dv_ref
            for e in range(RADIUS):
                lo_ref[which, e, 0, :, cols] = low[e * TILE : (e + 1) * TILE].astype(BF16)
                hi_ref[which, e, 0, :, cols] = high[(e + 4) * TILE : (e + 5) * TILE].astype(BF16)
            for e in range(FR_DEV):
                own = low[(e + 2) * TILE : (e + 3) * TILE] + high[e * TILE : (e + 1) * TILE]
                own_ref[e, 0, :, cols] = own.astype(BF16)

    term = dot(at_ref[...], dm_ref[...], NT)

    @pl.when(t == 0)
    def _():
        acc_ref[...] = term

    @pl.when(t > 0)
    def _():
        acc_ref[...] += term

    @pl.when(t == NTILE - 1)
    def _():
        full = dot(acc_ref[...].astype(BF16), piece_order_t())
        for b in range(HL):
            r_ref[b] = full[b * BLK : (b + 1) * BLK, b * BLK : (b + 1) * BLK].astype(BF16)


def backward(q4, k4, v4, halos, rb, attn_t, probs, inv, dmix):
    out4 = jax.ShapeDtypeStruct(OUT4, BF16)
    halo = jax.ShapeDtypeStruct(HALO, BF16)
    end = (HL, BLK, BLK)
    return pl.pallas_call(
        backward_kernel,
        grid=(NTILE,),
        in_specs=[tile_spec(FR_DEV)] * 3
        + [tile_spec(RADIUS)] * 4
        + [whole((WID, WID)), col_spec(), p_spec(), inv_spec(), col_spec()],
        out_specs=[tile_spec(FR_DEV)] * 3 + [pair_spec()] * 2 + [whole(end)],
        out_shape=[out4] * 3 + [halo] * 2 + [jax.ShapeDtypeStruct(end, BF16)],
        scratch_shapes=[pltpu.VMEM((WID, WID), F32)],
        compiler_params=params(),
        cost_estimate=pl.CostEstimate(
            flops=12 * 10**9, bytes_accessed=30 * 10**6, transcendentals=0
        ),
        name="backward",
    )(q4, k4, v4, *halos, rb, attn_t, probs, inv, dmix)


def add_kernel(dk_ref, dv_ref, below_ref, above_ref, ok_ref, ov_ref):
    for which, (own, out) in enumerate(((dk_ref, ok_ref), (dv_ref, ov_ref))):
        for e in range(RADIUS):
            out[e] = (own[e].astype(F32) + below_ref[which, e].astype(F32)).astype(BF16)
            up = own[RADIUS + e].astype(F32) + above_ref[which, e].astype(F32)
            out[RADIUS + e] = up.astype(BF16)


def add_halos(dk, dv, below, above):
    return pl.pallas_call(
        add_kernel,
        grid=(NTILE,),
        in_specs=[tile_spec(FR_DEV)] * 2 + [pair_spec()] * 2,
        out_specs=[tile_spec(FR_DEV)] * 2,
        out_shape=[jax.ShapeDtypeStruct(OUT4, BF16)] * 2,
        compiler_params=params(16),
        cost_estimate=pl.CostEstimate(flops=10**6, bytes_accessed=10 * 10**6, transcendentals=0),
        name="add_halos",
    )(dk, dv, below, above)


def left_kernel(back_ref, arr_ref, g_ref, l_ref, acc_ref):
    t = pl.program_id(0)
    term = dot(arr_ref[...], g_ref[...].reshape(COLS, WID))

    @pl.when(t == 0)
    def _():
        acc_ref[...] = term

    @pl.when(t > 0)
    def _():
        acc_ref[...] += term

    @pl.when(t == NTILE - 1)
    def _():
        full = dot(back_ref[...], acc_ref[...].astype(BF16))
        for c in range(HL):
            l_ref[c] = full[c * BLK : (c + 1) * BLK, c * BLK : (c + 1) * BLK].astype(BF16)


def left_sum(back, arrived, g4):
    return pl.pallas_call(
        left_kernel,
        grid=(NTILE,),
        in_specs=[whole((WID, WID)), col_spec(), tile_spec(FR_DEV)],
        out_specs=whole((HL, BLK, BLK)),
        out_shape=jax.ShapeDtypeStruct((HL, BLK, BLK), BF16),
        scratch_shapes=[pltpu.VMEM((WID, WID), F32)],
        compiler_params=params(16),
        cost_estimate=pl.CostEstimate(flops=10**9, bytes_accessed=4 * 10**6, transcendentals=0),
        name="left_sum",
    )(back, arrived, g4)


def project_kernel(w_ref, arr_ref, _, out_ref):
    for n in range(2):
        part = arr_ref[:, n * 2 * TILE : (n + 1) * 2 * TILE]
        out = dot(part, w_ref[...], TN).astype(BF16)
        out_ref[2 * n : 2 * n + 2] = out.reshape(2, 1, TILE, WID)


def project(w, arrived, after):
    return pl.pallas_call(
        project_kernel,
        grid=(NTILE,),
        in_specs=[whole((WID, WID)), col_spec(), pl.BlockSpec(memory_space=pl.ANY)],
        out_specs=tile_spec(FR_DEV),
        out_shape=jax.ShapeDtypeStruct(OUT4, BF16),
        compiler_params=params(16),
        cost_estimate=pl.CostEstimate(flops=10**9, bytes_accessed=4 * 10**6, transcendentals=0),
        name="project",
    )(w, arrived, after)


def tm_sums(right, left, norm, projected, dk):
    count = lax.axis_size("tm")
    first = lax.axis_index("tm") % 2 == 0

    def moved(y, to):
        return lax.ppermute(y, "tm", [(i, to(i)) for i in range(count)])

    def along_x(by):
        return lambda i: (i // 8) * 8 + (i % 8 + 2 * by) % 8

    right = gate(right, projected)
    x = jnp.where(first, right, left).astype(F32)
    x = (x + moved(jnp.where(first, left, right), lambda i: i ^ 1).astype(F32)).astype(BF16)
    one, two, three = (moved(x, along_x(by)).astype(F32) for by in (1, 2, 3))
    x = ((x.astype(F32) + two) + (one + three)).astype(BF16)
    near = moved(x, lambda i: i ^ 1).astype(F32)
    far = gate(moved(x, lambda i: i ^ 8), dk).astype(F32)
    cross = moved(x, lambda i: i ^ 9).astype(F32)
    x, other = (x.astype(F32) + far) * norm, (near + cross) * norm
    return jnp.where(first, x, other), jnp.where(first, other, x)


def on_device(queries, keys, values, right_blocks, left_blocks, block_perm, reach, grad_out):
    rows, width = queries.shape
    count = lax.axis_size("tm")
    n_head = lax.axis_size("head")
    up = [(i, (i + 1) % count) for i in range(count)]
    down = [((i + 1) % count, i) for i in range(count)]
    shape4 = (FR_DEV, NTILE, TILE, width)
    q4, k4, v4, g4 = (x.reshape(shape4) for x in (queries, keys, values, grad_out))
    half = (RADIUS, NTILE, TILE, width)
    cut = RADIUS * NTILE * TILE
    halos = [
        lax.ppermute(keys[rows - cut :], "tm", up).reshape(half),
        lax.ppermute(keys[:cut], "tm", down).reshape(half),
        lax.ppermute(values[rows - cut :], "tm", up).reshape(half),
        lax.ppermute(values[:cut], "tm", down).reshape(half),
    ]
    w, d_arrived = prep(block_perm, left_blocks, g4)

    def exchange(x):
        y = lax.all_to_all(
            x.reshape(n_head, width // n_head, rows), "head", split_axis=0, concat_axis=0, tiled=True
        )
        return y.reshape(width, rows)

    dmix = exchange(d_arrived)
    rb, rbt, back = orders(block_perm, right_blocks)
    attn_t, probs, inv, mixed = forward(reach, q4, k4, v4, halos, rbt)
    arrived = exchange(mixed)
    dq, dk, dv, lo, hi, right_term = backward(q4, k4, v4, halos, rb, attn_t, probs, inv, dmix)
    below = lax.ppermute(hi, "tm", up)
    above = lax.ppermute(lo, "tm", down)
    left_term = left_sum(back, arrived, g4)
    projected = project(w, arrived, left_term)
    dk, dv = add_halos(dk, dv, below, above)
    norm = float(rows * count) ** (-0.5)
    d_right, d_left = tm_sums(right_term, left_term, norm, projected, dk)
    flat = (rows, width)
    return (
        projected.reshape(flat),
        dq.reshape(flat),
        dk.reshape(flat),
        dv.reshape(flat),
        d_right,
        d_left,
    )


def solution(mesh):
    in_specs = (
        P("tm", "head"),
        P("tm", "head"),
        P("tm", "head"),
        P("head", None, None),
        P("head", None, None),
        P(),
        P(),
        P("tm", "head"),
    )
    out_specs = (
        P("tm", "head"),
        P("tm", "head"),
        P("tm", "head"),
        P("tm", "head"),
        P("head", None, None),
        P("head", None, None),
    )
    return jax.shard_map(
        on_device, mesh=mesh, in_specs=in_specs, out_specs=out_specs, check_vma=False
    )
```
